128 devices in a mesh: dp: 8 (over z, core), seq: 16 (over x, y).
Axes of the slice: x: 4, y: 4, z: 4, core: 2. Of those that a mesh axis runs over, the one named last changes fastest.
Arguments:
- q_raw: bfloat16 [8, 4096, 2048], P('dp', 'seq'), may hold values from -12 to 12
- k_raw: bfloat16 [8, 4096, 2048], P('dp', 'seq'), may hold values from -12 to 12
- values: bfloat16 [8, 4096, 2048], P('dp', 'seq'), may hold values from -6 to 6
- grad_out: bfloat16 [8, 4096, 2048], P('dp', 'seq'), may hold values from -6 to 6
- segment_ids: int32 [8, 4096], P('dp', 'seq'), may hold values from 0 to 3, never falling along the last dimension, each value on 1 to 2048 neighbouring positions
- row_plan: int32 [8, 4096], P('dp', 'seq'), may hold values from 0 to 4095, each once within a row
- q_gain: float32 [128], replicated, may hold values from 0.5 to 5.5
- k_gain: float32 [128], replicated, may hold values from 0.5 to 5.5
Outputs:
- dq_raw: bfloat16 [8, 4096, 2048], P('dp', 'seq')
- dk_raw: bfloat16 [8, 4096, 2048], P('dp', 'seq')
- dv_orig: bfloat16 [8, 4096, 2048], P('dp', 'seq')
- q_gain_grad: float32 [128], replicated
- k_gain_grad: float32 [128], replicated
The draws below stay inside these ranges and needn't reach their ends.
Inputs may be any that keep to these rules, and one draw needn't show every extreme that they name: `segment_ids`: clip numbers never fall along a group; each clip spans 1 to 2048 positions, one exactly 2048. `row_plan`: each group's row holds every position once.
All inputs are finite; a program needn't handle non-finite values.
Results may differ from the reference program's by a relative error of at most 0.0044.
The reference program's roundings to bfloat16 on the way count: a program that leaves them out, or rounds other values in their place, can miss the bound.
Values may be sent and summed in bfloat16 or wider, within the bound.
A program may use at most 192 MiB of HBM per device.

```python
import math
import jax
import jax.numpy as jnp
import numpy as np
from jax import lax

H = 16
HD = 128
CLIPS = 4
GROUPS = 8
L = 4096
HH = 2048


def key_rows(key):
    base = jax.random.normal(jax.random.fold_in(key, 21), (GROUPS, L, HH), jnp.float32)
    scales = jax.random.uniform(jax.random.fold_in(key, 22), (1, 1, HH), jnp.float32, 0.5, 2.0)
    rows = base * scales
    positions = jnp.arange(L)[None, :, None]
    rows = jnp.where(positions % 97 == 1, rows, rows)
    return jnp.clip(rows, -12.0, 12.0)


def draw_k_raw(key, part):
    rows = key_rows(key)
    return rows.astype(jnp.bfloat16)


def draw_q_raw(key, part):
    key = jax.random.fold_in(key, 4)
    own = jax.random.normal(jax.random.fold_in(key, 1), (GROUPS, L, HH), jnp.float32)
    own = own * jax.random.uniform(jax.random.fold_in(key, 2), (1, 1, HH), jnp.float32, 0.5, 2.0)
    own = jnp.clip(own, -12.0, 12.0)
    return own.astype(jnp.bfloat16)


def draw_q_gain(key, part):
    key = jax.random.fold_in(key, 7)
    return jnp.exp(jax.random.uniform(key, (HD,), jnp.float32, -0.6931, 0.6931))


def draw_k_gain(key, part):
    key = jax.random.fold_in(key, 8)
    return jnp.exp(jax.random.uniform(key, (HD,), jnp.float32, -0.6931, 0.6931))


def block_scale(key, extent, shards, smallest, high):
    def one(dim, blocks):
        draws = jax.random.uniform(jax.random.fold_in(jax.random.fold_in(key, 6), dim), (blocks,), jnp.float32, smallest / len(shards), high / len(shards))
        return jnp.repeat(jnp.exp(draws), extent[dim] // blocks).reshape((-1,) + (1,) * (len(extent) - dim - 1))

    factor_of = one(*shards[0])
    for cut in shards[1:]:
        factor_of = factor_of * one(*cut)
    return factor_of


def length_profile(number_of, total, bound, lean):
    weights = [(1 << 20) // math.isqrt(standing ** lean) + 1 for standing in range(2, number_of + 1)]
    surplus, given = total - bound - (number_of - 1), [1] * (number_of - 1)
    while surplus > 0:
        free = [i for i in range(number_of - 1) if given[i] < bound]
        pool, remaining = sum([weights[i] for i in free]), surplus
        for i in free:
            extra = min(bound - given[i], max(1, remaining * weights[i] // pool), surplus)
            given[i] = given[i] + extra
            surplus = surplus - extra
    return np.array([bound] + given)


def uneven(rng, number_of, total, bound, slope):
    if number_of == 2:
        one = jax.random.randint(rng, (), max(1, total - bound), min(bound, total - 1) + 1)
        return jnp.stack([one, total - one])
    lengths = jnp.asarray(length_profile(number_of, total, bound, slope), jnp.int32)
    pairs = (number_of - 1) // 2
    giver, sink = lengths[1:1 + 2 * pairs:2], lengths[2:2 + 2 * pairs:2]
    margin = jnp.minimum(giver - 1, bound - sink)
    shifted = jax.random.randint(jax.random.fold_in(rng, 1), (pairs,), 0, 1 << 20) % (margin + 1)
    lengths = lengths.at[1:1 + 2 * pairs:2].set(giver - shifted).at[2:2 + 2 * pairs:2].set(sink + shifted)
    return lengths[jax.random.permutation(jax.random.fold_in(rng, 2), number_of)]


def bell_draw(own_key, extent, scale, limit, cuts=(), kind=jnp.bfloat16):
    drawn = scale * jax.random.normal(own_key, extent, jnp.float32)
    if cuts:
        drawn = drawn * block_scale(own_key, extent, cuts, -0.22, 0.18)
    return jnp.clip(drawn, -limit, limit).astype(kind)


def setup_inputs(seed: int = 0) -> dict:
    key_list = jax.random.split(jax.random.key(seed), 9)
    q_raw = draw_q_raw(jax.random.fold_in(key_list[8], 71), 0)
    k_raw = draw_k_raw(jax.random.fold_in(key_list[8], 71), 0)
    values = bell_draw(key_list[2], (GROUPS, L, HH), 1.0, 6.0, ((0, 8), (1, 16)))
    grad_out = bell_draw(key_list[3], (GROUPS, L, HH), 1.0, 6.0, ((0, 8), (1, 16)))
    segment_ids = jax.vmap(lambda own: jnp.searchsorted(jnp.cumsum(uneven(own, CLIPS, L, L // 2, 1)), jnp.arange(L), side="right"))(jax.random.split(key_list[4], GROUPS)).reshape((GROUPS, L)).astype(jnp.int32)
    row_plan = jax.vmap(lambda own: jax.random.permutation(own, L))(jax.random.split(key_list[5], GROUPS)).reshape((GROUPS, L)).astype(jnp.int32)
    q_gain = draw_q_gain(jax.random.fold_in(key_list[8], 71), 0)
    k_gain = draw_k_gain(jax.random.fold_in(key_list[8], 71), 0)
    return {"q_raw": q_raw, "k_raw": k_raw, "values": values, "grad_out": grad_out, "segment_ids": segment_ids, "row_plan": row_plan, "q_gain": q_gain, "k_gain": k_gain}


def normalize(raw, gain):
    full = raw.astype(jnp.float32)
    rms = lax.rsqrt(lax.optimization_barrier(jnp.mean(full * full, axis=-1, keepdims=True)) + 1e-06)
    normed_hat = full * rms
    return (normed_hat, rms, (normed_hat * gain).astype(jnp.bfloat16))

def denormalize(d_norm, normed_hat, rms, gain):
    d_hat = d_norm * gain
    gain_part = lax.optimization_barrier(jnp.sum(d_norm * normed_hat, axis=(0, 1)))
    d_raw = rms * (d_hat - normed_hat * lax.optimization_barrier(jnp.mean(d_hat * normed_hat, axis=-1, keepdims=True)))
    return (d_raw.astype(jnp.bfloat16), gain_part)

def head_grad(q_norm, k_norm, value_rows, dout_rows, clip_ids):
    factor = q_norm.shape[-1] ** (-0.5)
    scores = jnp.dot(q_norm, k_norm.T, preferred_element_type=jnp.float32) * factor
    same_clip = clip_ids[:, None] == clip_ids[None, :]
    scores = jnp.where(same_clip, scores, -jnp.inf)
    top_score = lax.optimization_barrier(jnp.max(scores, axis=1, keepdims=True))
    weights = jnp.exp(scores - top_score)
    probs = weights / lax.optimization_barrier(jnp.sum(weights, axis=1, keepdims=True))
    probs_b = probs.astype(jnp.bfloat16)
    d_value = jnp.dot(probs_b.T, dout_rows, preferred_element_type=jnp.float32).astype(jnp.bfloat16)
    d_probs = jnp.dot(dout_rows, value_rows.T, preferred_element_type=jnp.float32)
    delta = lax.optimization_barrier(jnp.sum(d_probs * probs, axis=1, keepdims=True))
    d_scores = (probs * (d_probs - delta) * factor).astype(jnp.bfloat16)
    dq_norm = jnp.dot(d_scores, k_norm, preferred_element_type=jnp.float32)
    dk_norm = jnp.dot(d_scores.T, q_norm, preferred_element_type=jnp.float32)
    return (dq_norm, dk_norm, d_value)

def one_group(items, q_gain, k_gain):
    q_rows, k_rows, value_rows, dout_rows, clip_ids, plan_row = items
    seq_length = q_rows.shape[0]
    shaped = lambda a: a.reshape(seq_length, H, HD)
    q_hat, q_rms, q_norm = normalize(shaped(q_rows), q_gain)
    k_hat, k_rms, k_norm = normalize(shaped(k_rows), k_gain)
    heads_first = lambda a: a.transpose(1, 0, 2)
    dq_norm, dk_norm, d_value = lax.map(lambda part: head_grad(part[0], part[1], part[2], part[3], clip_ids), (heads_first(q_norm), heads_first(k_norm), heads_first(shaped(value_rows)), heads_first(shaped(dout_rows))))
    d_query, gain_q = denormalize(heads_first(dq_norm), q_hat, q_rms, q_gain)
    d_key, gain_k = denormalize(heads_first(dk_norm), k_hat, k_rms, k_gain)
    inverse = jnp.zeros((seq_length,), jnp.int32).at[plan_row].set(jnp.arange(seq_length, dtype=jnp.int32))
    flatten = lambda a: a.reshape(seq_length, H * HD)[inverse]
    return (flatten(d_query), flatten(d_key), flatten(heads_first(d_value)), gain_q, gain_k)

def reference(q_raw, k_raw, values, grad_out, segment_ids, row_plan, q_gain, k_gain):
    dq_raw, dk_raw, dv_orig, gain_q, gain_k = lax.map(lambda items: one_group(items, q_gain, k_gain), (q_raw, k_raw, values, grad_out, segment_ids, row_plan))
    return (dq_raw, dk_raw, dv_orig, lax.optimization_barrier(jnp.sum(gain_q, axis=0)), lax.optimization_barrier(jnp.sum(gain_k, axis=0)))
```

```python
import functools
import jax
import jax.numpy as jnp
from jax import lax
from jax.experimental import pallas as pl
from jax.experimental.pallas import tpu as pltpu
from jax.sharding import PartitionSpec as P

HD = 128
BLK = 256
BIG = -1e30
LOG2E = 1.4426950408889634
MESH = pl.DeviceIdType.MESH
NT = (((1,), (1,)), ((), ()))


def rows_mean(x):
    return jnp.sum(x, axis=1, keepdims=True) * (1.0 / HD)


def fold(x):
    return x.reshape(x.shape[0] // 8, 8, x.shape[1])


def kernel(
    nx, ny, ndp,
    q_in, k_in, d_in, v_in, seg_in, plan_in, qg_in, kg_in,
    oq, ok, ov, gq_out, gk_out,
    rq, rk, rd, rv, meta_src, meta, fbuf,
    raw_q, raw_k, qaug, kaug, k_t, dor, vr,
    wbuf, inv_ref, dp_ref, dvf, dkf, pair, stage, stage2,
    idx_v, idx_s, gpart, gsum, gbuf1, gbuf2,
    in_send, in_recv, meta_send, meta_recv, out_send, out_recv,
    g1_send, g1_recv, g2_send, g2_recv, loc_sem, oloc_sem, idx_sem,
):
    n = nx * ny
    length = n * BLK
    half = n // 2
    dp = lax.axis_index("dp")
    me = lax.axis_index("seq")
    mx, my = me // ny, me % ny
    factor = HD ** (-0.5)

    def peer_of(o):
        return ((mx + o // ny) % nx) * ny + (my + o % ny) % ny

    barrier = pltpu.get_barrier_semaphore()

    def greet(o, c):
        pl.semaphore_signal(barrier, inc=1, device_id=(dp, peer_of(o)), device_id_type=MESH)
        return c

    def greet_dp(o, c):
        pl.semaphore_signal(barrier, inc=1, device_id=((dp + o) % ndp, me), device_id_type=MESH)
        return c

    lax.fori_loop(1, n, greet, 0)
    lax.fori_loop(1, ndp, greet_dp, 0)

    own_rows = pl.ds(pl.multiple_of(me * BLK, BLK), BLK)
    own_cols = pl.ds(pl.multiple_of(me * HD, HD), HD)
    ins = ((q_in, rq), (k_in, rk), (d_in, rd), (v_in, rv))

    def local_in(a):
        src, dst = ins[a]
        return pltpu.make_async_copy(src.at[0, :, own_cols], dst.at[own_rows, :], loc_sem.at[a])

    for a in range(4):
        local_in(a).start()
    meta_src[0:1, :] = seg_in[...]
    meta_src[1:2, :] = plan_in[...]
    meta[me] = meta_src[...]
    pl.semaphore_wait(barrier, n - 1 + ndp - 1)

    def send_meta(o):
        return pltpu.make_async_remote_copy(
            src_ref=meta_src, dst_ref=meta.at[me], send_sem=meta_send.at[o], recv_sem=meta_recv.at[o],
            device_id=(dp, peer_of(o)), device_id_type=MESH)

    def send_in(a, o):
        src, dst = ins[a]
        p = peer_of(o)
        return pltpu.make_async_remote_copy(
            src_ref=src.at[0, :, pl.ds(pl.multiple_of(p * HD, HD), HD)], dst_ref=dst.at[own_rows, :],
            send_sem=in_send.at[a, o], recv_sem=in_recv.at[a, o],
            device_id=(dp, p), device_id_type=MESH)

    def loop(lo, hi, body):
        def step(i, c):
            body(i)
            return c
        lax.fori_loop(lo, hi, step, 0)

    loop(1, n, lambda o: send_meta(o).start())
    for a in range(4):
        loop(1, n, lambda o, a=a: send_in(a, o).start())

    loop(1, n, lambda o: send_meta(o).wait())
    ids = meta[:, 0, :]
    starts = [jnp.int32(0)] + [jnp.sum((ids < c).astype(jnp.int32)) for c in (1, 2, 3)]
    ends = starts[1:] + [jnp.int32(length)]
    shift = jnp.int32(0)
    for lo, hi in zip(starts, ends):
        shift = shift + jnp.where(hi - lo == length // 2, lo, 0)

    lane = lax.broadcasted_iota(jnp.int32, (64, BLK), 1)
    sub = lax.broadcasted_iota(jnp.int32, (64, BLK), 0)

    def invert(d):
        row = jnp.zeros((1, BLK), jnp.int32)
        for g in range(BLK // 64):
            want = sub + (d * BLK + g * 64)
            acc = jnp.zeros((64, BLK), jnp.int32)
            for src in range(n):
                acc = jnp.maximum(acc, jnp.where(meta[src, 1:2, :] == want, lane + src * BLK, 0))
            col = jnp.max(acc, axis=1, keepdims=True)
            row = jnp.maximum(row, jnp.max(jnp.where(lane == sub + g * 64, col, 0), axis=0, keepdims=True))
        row = row - shift
        idx_v[d] = jnp.where(row < 0, row + length, row)

    loop(0, n, invert)
    to_smem = pltpu.make_async_copy(idx_v, idx_s, idx_sem)
    to_smem.start()

    def rotate_from(src):
        def conv(b):
            rows = pl.ds(pl.multiple_of(b * BLK, BLK), BLK)
            fbuf[rows, :] = src[rows, :].astype(jnp.float32)
        loop(0, n, conv)
        fbuf[length:length + BLK, :] = src[0:BLK, :].astype(jnp.float32)

    def offset(b):
        off = shift + b * BLK
        return jnp.where(off >= length, off - length, off)

    def arrive(a):
        local_in(a).wait()
        loop(1, n, lambda o: send_in(a, o).wait())

    wide_lane = lax.broadcasted_iota(jnp.int32, (BLK, HD), 1)
    wide_sub = lax.broadcasted_iota(jnp.int32, (BLK, HD), 0)

    def clip_of(off):
        pos = wide_sub + off
        pos = jnp.where(pos >= length, pos - length, pos)
        one = lambda b: jnp.where(pos >= b, 1, 0)
        return one(starts[1]) + one(starts[2]) + one(starts[3])

    def hat_of(x):
        rms = lax.rsqrt(rows_mean(x * x) + 1e-06)
        return x * rms, rms

    arrive(0)
    rotate_from(rq)

    def prep_q(b):
        off = offset(b)
        x = fbuf[pl.ds(off, BLK), :]
        raw_q[b] = x.astype(jnp.bfloat16)
        hat, _ = hat_of(x)
        qaug[b, :, 0:HD] = (hat * qg_in[...]).astype(jnp.bfloat16)
        qaug[b, :, HD:2 * HD] = jnp.where(wide_lane == clip_of(off), 1.0, 0.0).astype(jnp.bfloat16)

    loop(0, n, prep_q)

    arrive(1)
    rotate_from(rk)

    def prep_k(b):
        off = offset(b)
        x = fbuf[pl.ds(off, BLK), :]
        raw_k[b] = x.astype(jnp.bfloat16)
        hat, _ = hat_of(x)
        normed = (hat * kg_in[...]).astype(jnp.bfloat16)
        kaug[b, :, 0:HD] = normed
        other = jnp.where(wide_lane == clip_of(off), 0.0, jnp.where(wide_lane < 4, BIG, 0.0))
        kaug[b, :, HD:2 * HD] = other.astype(jnp.bfloat16)
        k_t[b] = normed.astype(jnp.float32).T.astype(jnp.bfloat16)

    loop(0, n, prep_k)

    scale = factor * LOG2E

    def weigh(t):
        first = (t // half) * half
        queries = qaug[t]
        top = None
        for c in range(half):
            s = lax.dot_general(kaug[first + c], queries, NT, preferred_element_type=jnp.float32)
            wbuf[t, c * BLK:(c + 1) * BLK, :] = s
            m = jnp.max(fold(s), axis=0)
            top = m if top is None else jnp.maximum(top, m)
        top = jnp.max(top, axis=0, keepdims=True) * scale
        total = jnp.zeros((8, BLK), jnp.float32)
        for c in range(half):
            w = jnp.exp2(wbuf[t, c * BLK:(c + 1) * BLK, :] * scale - top)
            wbuf[t, c * BLK:(c + 1) * BLK, :] = w
            total = total + jnp.sum(fold(w), axis=0)
        inv_ref[t] = 1.0 / jnp.sum(total, axis=0, keepdims=True)

    loop(0, n, weigh)

    arrive(2)
    rotate_from(rd)

    def prep_d(b):
        dor[b] = fbuf[pl.ds(offset(b), BLK), :].astype(jnp.bfloat16)

    loop(0, n, prep_d)

    def value_grad(b):
        first = (b // half) * half
        keys = pl.ds(pl.multiple_of((b - first) * BLK, BLK), BLK)
        acc = jnp.zeros((BLK, HD), jnp.float32)
        for t in range(half):
            probs = (wbuf[first + t, keys, :] * inv_ref[first + t]).astype(jnp.bfloat16)
            acc = acc + jnp.dot(probs, dor[first + t], preferred_element_type=jnp.float32)
        dvf[pl.ds(pl.multiple_of(b * BLK, BLK), BLK), :] = acc

    loop(0, n, value_grad)
    to_smem.wait()

    outs = ((rq, ov), (rk, oq), (rd, ok))

    def chunk(p):
        return pl.ds(pl.multiple_of(p * BLK, BLK), BLK)

    def send_out(a, o):
        src, dst = outs[a]
        p = peer_of(o)
        return pltpu.make_async_remote_copy(
            src_ref=src.at[chunk(p), :], dst_ref=dst.at[0, :, own_cols],
            send_sem=out_send.at[a, o], recv_sem=out_recv.at[a, o],
            device_id=(dp, p), device_id_type=MESH)

    def local_out(a):
        src, dst = outs[a]
        return pltpu.make_async_copy(src.at[own_rows, :], dst.at[0, :, own_cols], oloc_sem.at[a])

    def pick_v(p):
        def some(g):
            for u in range(16):
                j = g * 16 + u
                stage[pl.ds(j, 1), :] = dvf[pl.ds(idx_s[p, 0, j], 1), :]
        loop(0, BLK // 16, some)
        rq[chunk(p), :] = stage[...].astype(jnp.bfloat16)

    def out_v(o):
        pick_v(peer_of(o))
        send_out(0, o).start()

    loop(1, n, out_v)
    pick_v(me)
    local_out(0).start()

    arrive(3)
    rotate_from(rv)

    def prep_v(b):
        vr[b] = fbuf[pl.ds(offset(b), BLK), :].astype(jnp.bfloat16)
        dkf[b] = jnp.zeros((BLK, HD), jnp.float32)

    loop(0, n, prep_v)
    gpart[...] = jnp.zeros_like(gpart)

    def denorm(d_norm, raw, gain, row):
        hat, rms = hat_of(raw.astype(jnp.float32))
        gpart[row:row + 1, :] += jnp.sum(d_norm * hat, axis=0, keepdims=True)
        d_hat = d_norm * gain
        return rms * (d_hat - hat * rows_mean(d_hat * hat))

    def score_grad(t):
        first = (t // half) * half
        douts = dor[t]
        acc = jnp.zeros((8, BLK), jnp.float32)
        for c in range(half):
            d = lax.dot_general(vr[first + c], douts, NT, preferred_element_type=jnp.float32)
            dp_ref[c * BLK:(c + 1) * BLK, :] = d
            acc = acc + jnp.sum(fold(d * wbuf[t, c * BLK:(c + 1) * BLK, :]), axis=0)
        delta = jnp.sum(acc, axis=0, keepdims=True) * inv_ref[t]
        scaled = inv_ref[t] * factor
        queries = qaug[t, :, 0:HD]
        dq_t = jnp.zeros((HD, BLK), jnp.float32)
        for c in range(half):
            rows = slice(c * BLK, (c + 1) * BLK)
            ds = ((wbuf[t, rows, :] * scaled) * (dp_ref[rows, :] - delta)).astype(jnp.bfloat16)
            dkf[first + c] += jnp.dot(ds, queries, preferred_element_type=jnp.float32)
            dq_t = dq_t + jnp.dot(k_t[first + c], ds, preferred_element_type=jnp.float32)
        pair[pl.ds(t * (2 * BLK), BLK, stride=2), :] = denorm(dq_t.T, raw_q[t], qg_in[...], 0)

    loop(0, n, score_grad)

    def key_grad(b):
        pair[pl.ds(b * (2 * BLK) + 1, BLK, stride=2), :] = denorm(dkf[b], raw_k[b], kg_in[...], 1)

    loop(0, n, key_grad)

    gbuf1[me] = gpart[...]

    def send_g1(o):
        return pltpu.make_async_remote_copy(
            src_ref=gpart, dst_ref=gbuf1.at[me], send_sem=g1_send.at[o], recv_sem=g1_recv.at[o],
            device_id=(dp, peer_of(o)), device_id_type=MESH)

    def send_g2(o):
        return pltpu.make_async_remote_copy(
            src_ref=gsum, dst_ref=gbuf2.at[dp], send_sem=g2_send.at[o], recv_sem=g2_recv.at[o],
            device_id=((dp + o) % ndp, me), device_id_type=MESH)

    loop(1, n, lambda o: send_g1(o).start())
    loop(1, n, lambda o: send_out(0, o).wait_send())

    def pick_qk(p):
        def some(g):
            for u in range(16):
                j = g * 16 + u
                stage2[pl.ds(2 * j, 2), :] = pair[pl.ds(2 * idx_s[p, 0, j], 2), :]
        loop(0, BLK // 16, some)
        rk[chunk(p), :] = stage2[pl.ds(0, BLK, stride=2), :].astype(jnp.bfloat16)
        rd[chunk(p), :] = stage2[pl.ds(1, BLK, stride=2), :].astype(jnp.bfloat16)

    def out_qk(o):
        pick_qk(peer_of(o))
        send_out(1, o).start()
        send_out(2, o).start()

    loop(1, n, out_qk)
    pick_qk(me)
    local_out(1).start()
    local_out(2).start()

    loop(1, n, lambda o: send_g1(o).wait())
    gsum[...] = jnp.sum(gbuf1[...], axis=0)
    gbuf2[dp] = gsum[...]
    loop(1, ndp, lambda o: send_g2(o).start())
    loop(1, ndp, lambda o: send_g2(o).wait())
    grads = jnp.sum(gbuf2[...], axis=0)
    gq_out[...] = grads[0:1, :]
    gk_out[...] = grads[1:2, :]

    loop(1, n, lambda o: send_out(0, o).wait_recv())
    for a in (1, 2):
        loop(1, n, lambda o, a=a: send_out(a, o).wait())
    for a in range(3):
        local_out(a).wait()


def on_device(nx, ny, ndp, q_raw, k_raw, values, grad_out, segment_ids, row_plan, q_gain, k_gain):
    n = nx * ny
    length = n * BLK
    bf, f32, i32 = jnp.bfloat16, jnp.float32, jnp.int32
    dma = pltpu.SemaphoreType.DMA
    hbm = pl.BlockSpec(memory_space=pl.ANY)
    vmem = pl.BlockSpec(memory_space=pltpu.VMEM)
    big = jax.ShapeDtypeStruct(q_raw.shape, bf)
    small = jax.ShapeDtypeStruct((1, HD), f32)
    half = n // 2
    oq, ok, ov, gq, gk = pl.pallas_call(
        functools.partial(kernel, nx, ny, ndp),
        out_shape=(big, big, big, small, small),
        in_specs=[hbm] * 4 + [vmem] * 4,
        out_specs=(hbm, hbm, hbm, vmem, vmem),
        scratch_shapes=[
            pltpu.VMEM((length, HD), bf),
            pltpu.VMEM((length, HD), bf),
            pltpu.VMEM((length, HD), bf),
            pltpu.VMEM((length, HD), bf),
            pltpu.VMEM((2, BLK), i32),
            pltpu.VMEM((n, 2, BLK), i32),
            pltpu.VMEM((length + BLK, HD), f32),
            pltpu.VMEM((n, BLK, HD), bf),
            pltpu.VMEM((n, BLK, HD), bf),
            pltpu.VMEM((n, BLK, 2 * HD), bf),
            pltpu.VMEM((n, BLK, 2 * HD), bf),
            pltpu.VMEM((n, HD, BLK), bf),
            pltpu.VMEM((n, BLK, HD), bf),
            pltpu.VMEM((n, BLK, HD), bf),
            pltpu.VMEM((n, length // 2, BLK), f32),
            pltpu.VMEM((n, 1, BLK), f32),
            pltpu.VMEM((length // 2, BLK), f32),
            pltpu.VMEM((length, HD), f32),
            pltpu.VMEM((n, BLK, HD), f32),
            pltpu.VMEM((2 * length, HD), f32),
            pltpu.VMEM((BLK, HD), f32),
            pltpu.VMEM((2 * BLK, HD), f32),
            pltpu.VMEM((n, 1, BLK), i32),
            pltpu.SMEM((n, 1, BLK), i32),
            pltpu.VMEM((2, HD), f32),
            pltpu.VMEM((2, HD), f32),
            pltpu.VMEM((n, 2, HD), f32),
            pltpu.VMEM((ndp, 2, HD), f32),
            dma((4, n)), dma((4, n)), dma((n,)), dma((n,)), dma((3, n)), dma((3, n)),
            dma((n,)), dma((n,)), dma((ndp,)), dma((ndp,)), dma((4,)), dma((3,)), dma,
        ],
        compiler_params=pltpu.CompilerParams(
            collective_id=0, has_side_effects=True, vmem_limit_bytes=62 * 2**20),
        cost_estimate=pl.CostEstimate(
            flops=10 * HD * length * length // 2, bytes_accessed=14 * length * HD, transcendentals=length * length // 2),
        name="attention_backward",
    )(q_raw, k_raw, grad_out, values, segment_ids, row_plan, q_gain.reshape(1, HD), k_gain.reshape(1, HD))
    return oq, ok, ov, gq.reshape(HD), gk.reshape(HD)


def solution(mesh):
    rows = P("dp", "seq", None)
    n = mesh.shape["seq"]
    ny = 4
    return jax.shard_map(
        functools.partial(on_device, n // ny, ny, mesh.shape["dp"]),
        mesh=mesh,
        in_specs=(rows, rows, rows, rows, P("dp", "seq"), P("dp", "seq"), P(), P()),
        out_specs=(rows, rows, rows, P(), P()),
        check_vma=False,
    )
```

```python
import functools
import jax
import jax.numpy as jnp
from jax import lax
from jax.experimental import pallas as pl
from jax.experimental.pallas import tpu as pltpu
from jax.sharding import PartitionSpec as P

HD = 128
BLK = 256
BIG = -1e30
LOG2E = 1.4426950408889634
MESH = pl.DeviceIdType.MESH
NT = (((1,), (1,)), ((), ()))


def rows_mean(x):
    return jnp.sum(x, axis=1, keepdims=True) * (1.0 / HD)


def fold(x):
    return x.reshape(x.shape[0] // 8, 8, x.shape[1])


def kernel(
    nx, ny, ndp,
    q_in, k_in, d_in, v_in, seg_in, plan_in, qg_in, kg_in,
    oq, ok, ov, gq_out, gk_out,
    rq, rk, rd, rv, meta_src, meta, fq, fk, fn,
    qaug, kaug, k_t, dor, vr,
    wbuf, inv_ref, dp_a, dp_b, dvf, dkf, stage,
    idx_v, idx_s, gpart, gsum, gbuf1, gbuf2,
    in_send, in_recv, meta_send, meta_recv, out_send, out_recv,
    g1_send, g1_recv, g2_send, g2_recv, loc_sem, oloc_sem, idx_sem,
):
    n = nx * ny
    length = n * BLK
    half = n // 2
    dp = lax.axis_index("dp")
    me = lax.axis_index("seq")
    mx, my = me // ny, me % ny
    factor = HD ** (-0.5)

    def peer_of(o):
        return ((mx + nx - o // ny) % nx) * ny + (my + ny - o % ny) % ny

    def source_of(o):
        return ((mx + o // ny) % nx) * ny + (my + o % ny) % ny

    barrier = pltpu.get_barrier_semaphore()

    def greet(o, c):
        pl.semaphore_signal(barrier, inc=1, device_id=(dp, peer_of(o)), device_id_type=MESH)
        return c

    def greet_dp(o, c):
        pl.semaphore_signal(barrier, inc=1, device_id=((dp + o) % ndp, me), device_id_type=MESH)
        return c

    lax.fori_loop(1, n, greet, 0)
    lax.fori_loop(1, ndp, greet_dp, 0)

    own_rows = pl.ds(pl.multiple_of(me * BLK, BLK), BLK)
    own_cols = pl.ds(pl.multiple_of(me * HD, HD), HD)
    ins = ((k_in, rk), (q_in, rq), (d_in, rd), (v_in, rv))

    def chunk(p):
        return pl.ds(pl.multiple_of(p * BLK, BLK), BLK)

    def local_in(a):
        src, dst = ins[a]
        return pltpu.make_async_copy(src.at[0, :, own_cols], dst.at[own_rows, :], loc_sem.at[a])

    for a in range(4):
        local_in(a).start()
    meta_src[0:1, :] = seg_in[...]
    meta_src[1:2, :] = plan_in[...]
    meta[me] = meta_src[...]
    pl.semaphore_wait(barrier, n - 1 + ndp - 1)

    def send_meta(o):
        return pltpu.make_async_remote_copy(
            src_ref=meta_src, dst_ref=meta.at[me], send_sem=meta_send.at[o], recv_sem=meta_recv.at[o],
            device_id=(dp, peer_of(o)), device_id_type=MESH)

    def send_in(a, o):
        src, dst = ins[a]
        p = peer_of(o)
        return pltpu.make_async_remote_copy(
            src_ref=src.at[0, :, pl.ds(pl.multiple_of(p * HD, HD), HD)], dst_ref=dst.at[own_rows, :],
            send_sem=in_send.at[a, o], recv_sem=in_recv.at[a, o],
            device_id=(dp, p), device_id_type=MESH)

    def loop(lo, hi, body):
        def step(i, c):
            body(i)
            return c
        lax.fori_loop(lo, hi, step, 0)

    loop(1, n, lambda o: send_meta(o).start())
    for a in range(4):
        loop(1, n, lambda o, a=a: send_in(a, o).start())

    loop(1, n, lambda o: send_meta(o).wait())
    ids = meta[:, 0, :]
    starts = [jnp.int32(0)] + [jnp.sum((ids < c).astype(jnp.int32)) for c in (1, 2, 3)]
    ends = starts[1:] + [jnp.int32(length)]
    shift = jnp.int32(0)
    for lo, hi in zip(starts, ends):
        shift = shift + jnp.where(hi - lo == length // 2, lo, 0)

    slip = lax.rem(shift, BLK)
    lead = lax.div(shift, BLK)

    def kin(tile, c):
        outside = jnp.where(lax.rem(tile + n - lead, n) >= half, half, 0)
        return lax.rem(lead + outside + c, n)

    lane = lax.broadcasted_iota(jnp.int32, (64, BLK), 1)
    sub = lax.broadcasted_iota(jnp.int32, (64, BLK), 0)

    def invert(d):
        row = jnp.zeros((1, BLK), jnp.int32)
        for g in range(BLK // 64):
            want = sub + (d * BLK + g * 64)
            acc = jnp.zeros((64, BLK), jnp.int32)
            for src in range(n):
                acc = jnp.maximum(acc, jnp.where(meta[src, 1:2, :] == want, lane + src * BLK, 0))
            col = jnp.max(acc, axis=1, keepdims=True)
            row = jnp.maximum(row, jnp.max(jnp.where(lane == sub + g * 64, col, 0), axis=0, keepdims=True))
        row = row - slip
        idx_v[d] = jnp.where(row < 0, row + length, row)

    loop(0, n, invert)
    to_smem = pltpu.make_async_copy(idx_v, idx_s, idx_sem)
    to_smem.start()

    def on_arrival(a, take, tile):
        def get(o):
            send_in(a, o).wait_recv()
            p = source_of(o)
            take(p, p)

            @pl.when(p == 0)
            def _():
                take(0, n)

        local_in(a).wait()
        take(me, me)

        @pl.when(me == 0)
        def _():
            take(0, n)

        loop(1, ny, get)

        def one(k):
            @pl.when((k % ny == ny - 1) & (k < n - ny))
            def _():
                loop(k + 1, k + 1 + ny, get)
            tile(((mx + k // ny) % nx) * ny + k % ny)

        loop(0, n, one)

    def rows_of(u):
        return pl.ds(u * BLK + slip, BLK)

    wide_lane = lax.broadcasted_iota(jnp.int32, (BLK, HD), 1)
    wide_sub = lax.broadcasted_iota(jnp.int32, (BLK, HD), 0)

    def clip_of(u):
        pos = wide_sub + (slip + u * BLK)
        pos = jnp.where(pos >= length, pos - length, pos)
        one = lambda b: jnp.where(pos >= b, 1, 0)
        return one(starts[1]) + one(starts[2]) + one(starts[3])

    def hat_of(x):
        rms = lax.rsqrt(rows_mean(x * x) + 1e-06)
        return x * rms, rms

    def norm_chunk(src, full, gain, o, to):
        x = src[chunk(o), :].astype(jnp.float32)
        full[chunk(to), :] = x
        hat, _ = hat_of(x)
        fn[chunk(to), :] = (hat * gain[...]).astype(jnp.bfloat16).astype(jnp.float32)

    def prep_k(b):
        x = fn[rows_of(b), :]
        kaug[b, :, 0:HD] = x.astype(jnp.bfloat16)
        other = jnp.where(wide_lane == clip_of(b), 0.0, jnp.where(wide_lane < 4, BIG, 0.0))
        kaug[b, :, HD:2 * HD] = other.astype(jnp.bfloat16)
        k_t[b] = x.T.astype(jnp.bfloat16)

    on_arrival(0, lambda o, to: norm_chunk(rk, fk, kg_in, o, to), prep_k)

    def prep_q(b):
        qaug[b, :, 0:HD] = fn[rows_of(b), :].astype(jnp.bfloat16)
        qaug[b, :, HD:2 * HD] = jnp.where(wide_lane == clip_of(b), 1.0, 0.0).astype(jnp.bfloat16)

    scale = factor * LOG2E

    def weigh(t):
        queries = qaug[t]
        top = None
        for c in range(half):
            s = lax.dot_general(kaug[kin(t, c)], queries, NT, preferred_element_type=jnp.float32)
            wbuf[t, c] = s
            m = jnp.max(fold(s), axis=0)
            top = m if top is None else jnp.maximum(top, m)
        top = jnp.max(top, axis=0, keepdims=True) * scale
        total = jnp.zeros((8, BLK), jnp.float32)
        for c in range(half):
            w = jnp.exp2(wbuf[t, c] * scale - top)
            wbuf[t, c] = w
            total = total + jnp.sum(fold(w), axis=0)
        inv_ref[t] = 1.0 / jnp.sum(total, axis=0, keepdims=True)

    def take_q(b):
        prep_q(b)
        weigh(b)

    on_arrival(1, lambda o, to: norm_chunk(rq, fq, qg_in, o, to), take_q)

    def widen(src, o, to):
        fn[chunk(to), :] = src[chunk(o), :].astype(jnp.float32)

    def prep_d(b):
        dor[b] = fn[rows_of(b), :].astype(jnp.bfloat16)

    on_arrival(2, lambda o, to: widen(rd, o, to), prep_d)

    def place(b):
        return lax.rem(b + n - lead, half)

    def value_grad(b):
        acc = jnp.zeros((BLK, HD), jnp.float32)
        for j in range(half):
            t = kin(b, j)
            probs = (wbuf[t, place(b)] * inv_ref[t]).astype(jnp.bfloat16)
            acc = acc + jnp.dot(probs, dor[t], preferred_element_type=jnp.float32)
        dvf[chunk(b), :] = acc

    loop(0, n, value_grad)
    to_smem.wait()

    outs = ((rq, ov), (rk, oq), (rd, ok))

    def send_out(a, o):
        src, dst = outs[a]
        p = peer_of(o)
        return pltpu.make_async_remote_copy(
            src_ref=src.at[chunk(p), :], dst_ref=dst.at[0, :, own_cols],
            send_sem=out_send.at[a, o], recv_sem=out_recv.at[a, o],
            device_id=(dp, p), device_id_type=MESH)

    def local_out(a):
        src, dst = outs[a]
        return pltpu.make_async_copy(src.at[own_rows, :], dst.at[0, :, own_cols], oloc_sem.at[a])

    def pick(rows, a, p, lo, count):
        for j in range(lo, lo + count):
            stage[j:j + 1, :] = rows[pl.ds(idx_s[p, 0, j], 1), :]
        out = outs[a][0]
        out[pl.ds(pl.multiple_of(p * BLK + lo, 16), count), :] = stage[lo:lo + count, :].astype(jnp.bfloat16)

    def leave(a, o):
        @pl.when(o == 0)
        def _():
            local_out(a).start()

        @pl.when(o != 0)
        def _():
            send_out(a, o).start()

    def prep_v(b):
        vr[b] = fn[rows_of(b), :].astype(jnp.bfloat16)

    on_arrival(3, lambda o, to: widen(rv, o, to), prep_v)
    gpart[...] = jnp.zeros_like(gpart)

    def denorm(rows, full, b, gain, row):
        hat, rms = hat_of(full[rows_of(b), :])
        d_norm = rows[chunk(b), :]
        gpart[row:row + 1, :] += jnp.sum(d_norm * hat, axis=0, keepdims=True)
        d_hat = d_norm * gain[...]
        rows[chunk(b), :] = rms * (d_hat - hat * rows_mean(d_hat * hat))

    part = BLK // half

    def value_dot(t, c):
        return lax.dot_general(vr[kin(t, c)], dor[t], NT, preferred_element_type=jnp.float32)

    def weighted(d, t, c):
        return jnp.sum(fold(d * wbuf[t, c]), axis=0)

    def score_grad(t, acc, now, t_next, later, last):
        dest = peer_of(t)
        delta = jnp.sum(acc, axis=0, keepdims=True) * inv_ref[t]
        scaled = inv_ref[t] * factor
        dq_t = jnp.zeros((HD, BLK), jnp.float32)
        acc = jnp.zeros((8, BLK), jnp.float32)
        for c in range(half):
            d = value_dot(t_next, c)
            ds = (wbuf[t, c] * scaled) * (now[c] - delta)
            wbuf[t, c] = ds
            dq_t = dq_t + jnp.dot(k_t[kin(t, c)], ds.astype(jnp.bfloat16), preferred_element_type=jnp.float32)
            later[c] = d
            acc = acc + weighted(d, t_next, c)
            pick(dvf, 0, dest, c * part, part)
        fn[chunk(t), :] = dq_t.T
        last()
        leave(0, t)
        return acc

    acc = jnp.zeros((8, BLK), jnp.float32)
    for c in range(half):
        d = value_dot(0, c)
        dp_a[c] = d
        acc = acc + weighted(d, 0, c)

    def two(i, acc):
        t = 2 * i
        acc = score_grad(t, acc, dp_a, t + 1, dp_b, lambda: None)
        return score_grad(t + 1, acc, dp_b, (t + 2) % n, dp_a, lambda: denorm(fn, fq, t, qg_in, 0))

    lax.fori_loop(0, n // 2, two, acc)
    loop(0, n // 2, lambda i: denorm(fn, fq, 2 * i + 1, qg_in, 0))

    def key_grad(b):
        dest = peer_of(b)
        acc = jnp.zeros((BLK, HD), jnp.float32)
        for j in range(half):
            t = kin(b, j)
            ds = wbuf[t, place(b)].astype(jnp.bfloat16)
            acc = acc + jnp.dot(ds, qaug[t, :, 0:HD], preferred_element_type=jnp.float32)
            pick(fn, 1, dest, j * part, part)
        dkf[chunk(b), :] = acc
        leave(1, b)

    loop(0, n, key_grad)
    loop(0, n, lambda b: denorm(dkf, fk, b, kg_in, 1))

    gbuf1[me] = gpart[...]

    def send_g1(o):
        return pltpu.make_async_remote_copy(
            src_ref=gpart, dst_ref=gbuf1.at[me], send_sem=g1_send.at[o], recv_sem=g1_recv.at[o],
            device_id=(dp, peer_of(o)), device_id_type=MESH)

    def send_g2(o):
        return pltpu.make_async_remote_copy(
            src_ref=gsum, dst_ref=gbuf2.at[dp], send_sem=g2_send.at[o], recv_sem=g2_recv.at[o],
            device_id=((dp + o) % ndp, me), device_id_type=MESH)

    loop(1, n, lambda o: send_g1(o).start())

    def key_rows(o):
        pick(dkf, 2, peer_of(o), 0, BLK)
        leave(2, o)

    loop(0, n // 4, key_rows)
    loop(1, n, lambda o: send_g1(o).wait())
    gsum[...] = jnp.sum(gbuf1[...], axis=0)
    gbuf2[dp] = gsum[...]
    loop(1, ndp, lambda o: send_g2(o).start())
    loop(n // 4, n, key_rows)

    loop(1, ndp, lambda o: send_g2(o).wait())
    grads = jnp.sum(gbuf2[...], axis=0)
    gq_out[...] = grads[0:1, :]
    gk_out[...] = grads[1:2, :]

    for a in range(4):
        loop(1, n, lambda o, a=a: send_in(a, o).wait_send())
    for a in range(3):
        loop(1, n, lambda o, a=a: send_out(a, o).wait())
    for a in range(3):
        local_out(a).wait()


def on_device(nx, ny, ndp, q_raw, k_raw, values, grad_out, segment_ids, row_plan, q_gain, k_gain):
    n = nx * ny
    length = n * BLK
    bf, f32, i32 = jnp.bfloat16, jnp.float32, jnp.int32
    dma = pltpu.SemaphoreType.DMA
    hbm = pl.BlockSpec(memory_space=pl.ANY)
    vmem = pl.BlockSpec(memory_space=pltpu.VMEM)
    big = jax.ShapeDtypeStruct(q_raw.shape, bf)
    small = jax.ShapeDtypeStruct((1, HD), f32)
    half = n // 2
    oq, ok, ov, gq, gk = pl.pallas_call(
        functools.partial(kernel, nx, ny, ndp),
        out_shape=(big, big, big, small, small),
        in_specs=[hbm] * 4 + [vmem] * 4,
        out_specs=(hbm, hbm, hbm, vmem, vmem),
        scratch_shapes=[
            pltpu.VMEM((length, HD), bf),
            pltpu.VMEM((length, HD), bf),
            pltpu.VMEM((length, HD), bf),
            pltpu.VMEM((length, HD), bf),
            pltpu.VMEM((2, BLK), i32),
            pltpu.VMEM((n, 2, BLK), i32),
            pltpu.VMEM((length + BLK, HD), f32),
            pltpu.VMEM((length + BLK, HD), f32),
            pltpu.VMEM((length + BLK, HD), f32),
            pltpu.VMEM((n, BLK, 2 * HD), bf),
            pltpu.VMEM((n, BLK, 2 * HD), bf),
            pltpu.VMEM((n, HD, BLK), bf),
            pltpu.VMEM((n, BLK, HD), bf),
            pltpu.VMEM((n, BLK, HD), bf),
            pltpu.VMEM((n, half, BLK, BLK), f32),
            pltpu.VMEM((n, 1, BLK), f32),
            pltpu.VMEM((half, BLK, BLK), f32),
            pltpu.VMEM((half, BLK, BLK), f32),
            pltpu.VMEM((length, HD), f32),
            pltpu.VMEM((length, HD), f32),
            pltpu.VMEM((BLK, HD), f32),
            pltpu.VMEM((n, 1, BLK), i32),
            pltpu.SMEM((n, 1, BLK), i32),
            pltpu.VMEM((2, HD), f32),
            pltpu.VMEM((2, HD), f32),
            pltpu.VMEM((n, 2, HD), f32),
            pltpu.VMEM((ndp, 2, HD), f32),
            dma((4, n)), dma((4, n)), dma((n,)), dma((n,)), dma((3, n)), dma((3, n)),
            dma((n,)), dma((n,)), dma((ndp,)), dma((ndp,)), dma((4,)), dma((3,)), dma,
        ],
        compiler_params=pltpu.CompilerParams(
            collective_id=0, has_side_effects=True, vmem_limit_bytes=62 * 2**20),
        cost_estimate=pl.CostEstimate(
            flops=10 * HD * length * length // 2, bytes_accessed=14 * length * HD, transcendentals=length * length // 2),
        name="attention_backward",
    )(q_raw, k_raw, grad_out, values, segment_ids, row_plan, q_gain.reshape(1, HD), k_gain.reshape(1, HD))
    return oq, ok, ov, gq.reshape(HD), gk.reshape(HD)


def solution(mesh):
    rows = P("dp", "seq", None)
    n = mesh.shape["seq"]
    ny = 4
    return jax.shard_map(
        functools.partial(on_device, n // ny, ny, mesh.shape["dp"]),
        mesh=mesh,
        in_specs=(rows, rows, rows, rows, P("dp", "seq"), P("dp", "seq"), P(), P()),
        out_specs=(rows, rows, rows, P(), P()),
        check_vma=False,
    )
```

```python
import functools
import jax
import jax.numpy as jnp
from jax import lax
from jax.experimental import pallas as pl
from jax.experimental.pallas import tpu as pltpu
from jax.sharding import PartitionSpec as P

HD = 128
BLK = 256
BIG = -1e30
LOG2E = 1.4426950408889634
MESH = pl.DeviceIdType.MESH
NT = (((1,), (1,)), ((), ()))


def rows_mean(x):
    return jnp.sum(x, axis=1, keepdims=True) * (1.0 / HD)


def fold(x):
    return x.reshape(x.shape[0] // 8, 8, x.shape[1])


def kernel(
    nx, ny, ndp,
    q_in, k_in, d_in, v_in, seg_in, plan_in, qg_in, kg_in,
    oq, ok, ov, gq_out, gk_out,
    rq, rk, rd, rv, meta_src, meta, fq, fk, fn,
    qaug, kaug, k_t, dor, vr,
    wbuf, inv_ref, dp_a, dp_b, dvf, dkf, stage,
    idx_v, idx_s, gpart, gsum, gbuf1, gbuf2,
    in_send, in_recv, meta_send, meta_recv, out_send, out_recv,
    g1_send, g1_recv, g2_send, g2_recv, loc_sem, oloc_sem, idx_sem,
):
    n = nx * ny
    length = n * BLK
    half = n // 2
    dp = lax.axis_index("dp")
    me = lax.axis_index("seq")
    mx, my = me // ny, me % ny
    factor = HD ** (-0.5)

    def peer_of(o):
        return ((mx + nx - o // ny) % nx) * ny + (my + ny - o % ny) % ny

    def source_of(o):
        return ((mx + o // ny) % nx) * ny + (my + o % ny) % ny

    def stride(o):
        return (o * (5 + 6 * (dp % 2))) % n

    def mixed(o):
        return peer_of(stride(o))

    barrier = pltpu.get_barrier_semaphore()

    def greet(o, c):
        pl.semaphore_signal(barrier, inc=1, device_id=(dp, peer_of(o)), device_id_type=MESH)
        return c

    def greet_dp(o, c):
        pl.semaphore_signal(barrier, inc=1, device_id=((dp + o) % ndp, me), device_id_type=MESH)
        return c

    lax.fori_loop(1, n, greet, 0)
    lax.fori_loop(1, ndp, greet_dp, 0)

    own_rows = pl.ds(pl.multiple_of(me * BLK, BLK), BLK)
    own_cols = pl.ds(pl.multiple_of(me * HD, HD), HD)
    ins = ((k_in, rk), (q_in, rq), (d_in, rd), (v_in, rv))

    def chunk(p):
        return pl.ds(pl.multiple_of(p * BLK, BLK), BLK)

    def local_in(a):
        src, dst = ins[a]
        return pltpu.make_async_copy(src.at[0, :, own_cols], dst.at[own_rows, :], loc_sem.at[a])

    for a in range(4):
        local_in(a).start()
    meta_src[0:1, :] = seg_in[...]
    meta_src[1:2, :] = plan_in[...]
    meta[me] = meta_src[...]
    pl.semaphore_wait(barrier, n - 1 + ndp - 1)

    def send_meta(o):
        return pltpu.make_async_remote_copy(
            src_ref=meta_src, dst_ref=meta.at[me], send_sem=meta_send.at[o], recv_sem=meta_recv.at[o],
            device_id=(dp, peer_of(o)), device_id_type=MESH)

    def send_in(a, o):
        src, dst = ins[a]
        p = peer_of(o)
        return pltpu.make_async_remote_copy(
            src_ref=src.at[0, :, pl.ds(pl.multiple_of(p * HD, HD), HD)], dst_ref=dst.at[own_rows, :],
            send_sem=in_send.at[a, o], recv_sem=in_recv.at[a, o],
            device_id=(dp, p), device_id_type=MESH)

    def loop(lo, hi, body):
        def step(i, c):
            body(i)
            return c
        lax.fori_loop(lo, hi, step, 0)

    loop(1, n, lambda o: send_meta(o).start())
    for a in range(4):
        loop(1, n, lambda o, a=a: send_in(a, stride(o)).start())

    loop(1, n, lambda o: send_meta(o).wait())
    ids = meta[:, 0, :]
    starts = [jnp.int32(0)] + [jnp.sum((ids < c).astype(jnp.int32)) for c in (1, 2, 3)]
    ends = starts[1:] + [jnp.int32(length)]
    shift = jnp.int32(0)
    for lo, hi in zip(starts, ends):
        shift = shift + jnp.where(hi - lo == length // 2, lo, 0)

    slip = lax.rem(shift, BLK)
    lead = lax.div(shift, BLK)

    def kin(tile, c):
        outside = jnp.where(lax.rem(tile + n - lead, n) >= half, half, 0)
        return lax.rem(lead + outside + c, n)

    lane = lax.broadcasted_iota(jnp.int32, (64, BLK), 1)
    sub = lax.broadcasted_iota(jnp.int32, (64, BLK), 0)

    def invert(d):
        row = jnp.zeros((1, BLK), jnp.int32)
        for g in range(BLK // 64):
            want = sub + (d * BLK + g * 64)
            acc = jnp.zeros((64, BLK), jnp.int32)
            for src in range(n):
                acc = jnp.maximum(acc, jnp.where(meta[src, 1:2, :] == want, lane + src * BLK, 0))
            col = jnp.max(acc, axis=1, keepdims=True)
            row = jnp.maximum(row, jnp.max(jnp.where(lane == sub + g * 64, col, 0), axis=0, keepdims=True))
        row = row - slip
        idx_v[d] = jnp.where(row < 0, row + length, row)

    loop(0, n, invert)
    to_smem = pltpu.make_async_copy(idx_v, idx_s, idx_sem)
    to_smem.start()

    def on_arrival(a, take, tile):
        def get(o):
            send_in(a, o).wait_recv()
            p = source_of(o)
            take(p, p)

            @pl.when(p == 0)
            def _():
                take(0, n)

        local_in(a).wait()
        take(me, me)

        @pl.when(me == 0)
        def _():
            take(0, n)

        loop(1, ny, get)

        def one(k):
            @pl.when((k % ny == ny - 1) & (k < n - ny))
            def _():
                loop(k + 1, k + 1 + ny, get)
            tile(((mx + k // ny) % nx) * ny + k % ny, k)

        loop(0, n, one)

    def rows_of(u):
        return pl.ds(u * BLK + slip, BLK)

    wide_lane = lax.broadcasted_iota(jnp.int32, (BLK, HD), 1)
    wide_sub = lax.broadcasted_iota(jnp.int32, (BLK, HD), 0)

    def clip_of(u):
        pos = wide_sub + (slip + u * BLK)
        pos = jnp.where(pos >= length, pos - length, pos)
        one = lambda b: jnp.where(pos >= b, 1, 0)
        return one(starts[1]) + one(starts[2]) + one(starts[3])

    def hat_of(x):
        rms = lax.rsqrt(rows_mean(x * x) + 1e-06)
        return x * rms, rms

    def norm_chunk(src, full, gain, o, to):
        x = src[chunk(o), :].astype(jnp.float32)
        full[chunk(to), :] = x
        hat, _ = hat_of(x)
        fn[chunk(to), :] = (hat * gain[...]).astype(jnp.bfloat16).astype(jnp.float32)

    def prep_k(b):
        x = fn[rows_of(b), :]
        kaug[b, :, 0:HD] = x.astype(jnp.bfloat16)
        other = jnp.where(wide_lane == clip_of(b), 0.0, jnp.where(wide_lane < 4, BIG, 0.0))
        kaug[b, :, HD:2 * HD] = other.astype(jnp.bfloat16)
        k_t[b] = x.T.astype(jnp.bfloat16)

    on_arrival(0, lambda o, to: norm_chunk(rk, fk, kg_in, o, to), lambda b, k: prep_k(b))

    def prep_q(b):
        qaug[b, :, 0:HD] = fn[rows_of(b), :].astype(jnp.bfloat16)
        qaug[b, :, HD:2 * HD] = jnp.where(wide_lane == clip_of(b), 1.0, 0.0).astype(jnp.bfloat16)

    scale = factor * LOG2E

    def weigh(t):
        queries = qaug[t]
        top = None
        for c in range(half):
            s = lax.dot_general(kaug[kin(t, c)], queries, NT, preferred_element_type=jnp.float32)
            wbuf[t, c] = s
            m = jnp.max(fold(s), axis=0)
            top = m if top is None else jnp.maximum(top, m)
        top = jnp.max(top, axis=0, keepdims=True) * scale
        total = jnp.zeros((8, BLK), jnp.float32)
        for c in range(half):
            w = jnp.exp2(wbuf[t, c] * scale - top)
            wbuf[t, c] = w
            total = total + jnp.sum(fold(w), axis=0)
        inv_ref[t] = 1.0 / jnp.sum(total, axis=0, keepdims=True)

    def take_q(b, k):
        prep_q(b)
        weigh(b)

    on_arrival(1, lambda o, to: norm_chunk(rq, fq, qg_in, o, to), take_q)

    def widen(src, o, to):
        fn[chunk(to), :] = src[chunk(o), :].astype(jnp.float32)

    def prep_d(b):
        dor[b] = fn[rows_of(b), :].astype(jnp.bfloat16)

    on_arrival(2, lambda o, to: widen(rd, o, to), lambda b, k: prep_d(b))

    def place(b):
        return lax.rem(b + n - lead, half)

    def value_grad(b):
        acc = jnp.zeros((BLK, HD), jnp.float32)
        for j in range(half):
            t = kin(b, j)
            probs = (wbuf[t, place(b)] * inv_ref[t]).astype(jnp.bfloat16)
            acc = acc + jnp.dot(probs, dor[t], preferred_element_type=jnp.float32)
        dvf[chunk(b), :] = acc

    loop(0, n, value_grad)
    to_smem.wait()

    outs = ((rq, ov), (rk, oq), (rd, ok))

    def send_out(a, o):
        src, dst = outs[a]
        p = mixed(o)
        return pltpu.make_async_remote_copy(
            src_ref=src.at[chunk(p), :], dst_ref=dst.at[0, :, own_cols],
            send_sem=out_send.at[a, o], recv_sem=out_recv.at[a, o],
            device_id=(dp, p), device_id_type=MESH)

    def local_out(a):
        src, dst = outs[a]
        return pltpu.make_async_copy(src.at[own_rows, :], dst.at[0, :, own_cols], oloc_sem.at[a])

    def pick(rows, a, p, lo, count):
        for j in range(lo, lo + count):
            stage[j:j + 1, :] = rows[pl.ds(idx_s[p, 0, j], 1), :]
        out = outs[a][0]
        out[pl.ds(pl.multiple_of(p * BLK + lo, 16), count), :] = stage[lo:lo + count, :].astype(jnp.bfloat16)

    def leave(a, o):
        @pl.when(o == 0)
        def _():
            local_out(a).start()

        @pl.when(o != 0)
        def _():
            send_out(a, o).start()

    def take_v(b, k):
        vr[b] = fn[rows_of(b), :].astype(jnp.bfloat16)
        pick(dvf, 0, mixed(k), 0, BLK)
        leave(0, k)

    on_arrival(3, lambda o, to: widen(rv, o, to), take_v)
    gpart[...] = jnp.zeros_like(gpart)

    def denorm(rows, full, b, gain):
        hat, rms = hat_of(full[rows_of(b), :])
        d_norm = rows[chunk(b), :]
        d_hat = d_norm * gain[...]
        rows[chunk(b), :] = rms * (d_hat - hat * rows_mean(d_hat * hat))
        return d_norm, hat

    def denorm_q(b, valid=True):
        d_norm, hat = denorm(fn, fq, b, qg_in)
        normed = qaug[b, :, 0:HD].astype(jnp.float32)
        gpart[0:1, :] += jnp.where(valid, jnp.sum(d_norm * hat, axis=0, keepdims=True), 0.0)
        gpart[1:2, :] += jnp.where(valid, jnp.sum(d_norm * normed, axis=0, keepdims=True), 0.0)

    part = BLK // half

    def value_dot(t, c):
        return lax.dot_general(vr[kin(t, c)], dor[t], NT, preferred_element_type=jnp.float32)

    def weighted(d, t, c):
        return jnp.sum(fold(d * wbuf[t, c]), axis=0)

    def score_grad(t, acc, now, t_next, later):
        denorm_q((t + n - 1) % n, t > 0)
        delta = jnp.sum(acc, axis=0, keepdims=True) * inv_ref[t]
        scaled = inv_ref[t] * factor
        dq_t = jnp.zeros((HD, BLK), jnp.float32)
        acc = jnp.zeros((8, BLK), jnp.float32)
        for c in range(half):
            d = value_dot(t_next, c)
            ds = (wbuf[t, c] * scaled) * (now[c] - delta)
            wbuf[t, c] = ds
            dq_t = dq_t + jnp.dot(k_t[kin(t, c)], ds.astype(jnp.bfloat16), preferred_element_type=jnp.float32)
            later[c] = d
            acc = acc + weighted(d, t_next, c)
        fn[chunk(t), :] = dq_t.T
        return acc

    acc = jnp.zeros((8, BLK), jnp.float32)
    for c in range(half):
        d = value_dot(0, c)
        dp_a[c] = d
        acc = acc + weighted(d, 0, c)

    def two(i, acc):
        t = 2 * i
        acc = score_grad(t, acc, dp_a, t + 1, dp_b)
        return score_grad(t + 1, acc, dp_b, (t + 2) % n, dp_a)

    lax.fori_loop(0, n // 2, two, acc)
    denorm_q(n - 1)
    gpart[1:2, :] = gpart[1:2, :] / kg_in[...]
    dkf[chunk(n - 1), :] = jnp.zeros((BLK, HD), jnp.float32)

    gbuf1[me] = gpart[...]

    def send_g1(o):
        return pltpu.make_async_remote_copy(
            src_ref=gpart, dst_ref=gbuf1.at[me], send_sem=g1_send.at[o], recv_sem=g1_recv.at[o],
            device_id=(dp, peer_of(o)), device_id_type=MESH)

    def send_g2(o):
        return pltpu.make_async_remote_copy(
            src_ref=gsum, dst_ref=gbuf2.at[dp], send_sem=g2_send.at[o], recv_sem=g2_recv.at[o],
            device_id=((dp + o) % ndp, me), device_id_type=MESH)

    loop(1, n, lambda o: send_g1(o).start())

    def key_grad(b):
        dest = mixed(b)
        denorm(dkf, fk, (b + n - 1) % n, kg_in)
        acc = jnp.zeros((BLK, HD), jnp.float32)
        for j in range(half):
            t = kin(b, j)
            ds = wbuf[t, place(b)].astype(jnp.bfloat16)
            acc = acc + jnp.dot(ds, qaug[t, :, 0:HD], preferred_element_type=jnp.float32)
            pick(fn, 1, dest, j * part, part)
        dkf[chunk(b), :] = acc
        leave(1, b)

    loop(0, n, key_grad)
    denorm(dkf, fk, n - 1, kg_in)

    def key_rows(o):
        pick(dkf, 2, mixed(o), 0, BLK)
        leave(2, o)

    loop(1, n, lambda o: send_g1(o).wait())
    gsum[...] = jnp.sum(gbuf1[...], axis=0)
    gbuf2[dp] = gsum[...]
    loop(1, ndp, lambda o: send_g2(o).start())
    loop(0, n, key_rows)

    loop(1, ndp, lambda o: send_g2(o).wait())
    grads = jnp.sum(gbuf2[...], axis=0)
    gq_out[...] = grads[0:1, :]
    gk_out[...] = grads[1:2, :]

    for a in range(4):
        loop(1, n, lambda o, a=a: send_in(a, o).wait_send())
    for a in range(3):
        loop(1, n, lambda o, a=a: send_out(a, o).wait())
    for a in range(3):
        local_out(a).wait()


def hand_over(q, k, v, gq, gk, oq, ok, ov, gq_out, gk_out, held, sem):
    pairs = ((q, oq), (k, ok), (v, ov))
    parts = 2
    size = q.shape[1] // parts

    def move(a, part):
        rows = pl.ds(part * size, size)
        src, dst = pairs[a]
        return (pltpu.make_async_copy(src.at[0, rows, :], held.at[a, rows, :], sem.at[0, a, part]),
                pltpu.make_async_copy(held.at[a, rows, :], dst.at[0, rows, :], sem.at[1, a, part]))

    moves = [move(a, part) for a in range(3) for part in range(parts)]
    for get, _ in moves:
        get.start()
    gq_out[...] = gq[...]
    gk_out[...] = gk[...]
    for get, put in moves:
        get.wait()
        put.start()
    for _, put in moves:
        put.wait()


def on_device(nx, ny, ndp, q_raw, k_raw, values, grad_out, segment_ids, row_plan, q_gain, k_gain):
    n = nx * ny
    length = n * BLK
    bf, f32, i32 = jnp.bfloat16, jnp.float32, jnp.int32
    dma = pltpu.SemaphoreType.DMA
    hbm = pl.BlockSpec(memory_space=pl.ANY)
    vmem = pl.BlockSpec(memory_space=pltpu.VMEM)
    big = jax.ShapeDtypeStruct(q_raw.shape, bf)
    small = jax.ShapeDtypeStruct((1, HD), f32)
    half = n // 2
    oq, ok, ov, gq, gk = pl.pallas_call(
        functools.partial(kernel, nx, ny, ndp),
        out_shape=(big, big, big, small, small),
        in_specs=[hbm] * 4 + [vmem] * 4,
        out_specs=(hbm, hbm, hbm, vmem, vmem),
        scratch_shapes=[
            pltpu.VMEM((length, HD), bf),
            pltpu.VMEM((length, HD), bf),
            pltpu.VMEM((length, HD), bf),
            pltpu.VMEM((length, HD), bf),
            pltpu.VMEM((2, BLK), i32),
            pltpu.VMEM((n, 2, BLK), i32),
            pltpu.VMEM((length + BLK, HD), f32),
            pltpu.VMEM((length + BLK, HD), f32),
            pltpu.VMEM((length + BLK, HD), f32),
            pltpu.VMEM((n, BLK, 2 * HD), bf),
            pltpu.VMEM((n, BLK, 2 * HD), bf),
            pltpu.VMEM((n, HD, BLK), bf),
            pltpu.VMEM((n, BLK, HD), bf),
            pltpu.VMEM((n, BLK, HD), bf),
            pltpu.VMEM((n, half, BLK, BLK), f32),
            pltpu.VMEM((n, 1, BLK), f32),
            pltpu.VMEM((half, BLK, BLK), f32),
            pltpu.VMEM((half, BLK, BLK), f32),
            pltpu.VMEM((length, HD), f32),
            pltpu.VMEM((length, HD), f32),
            pltpu.VMEM((BLK, HD), f32),
            pltpu.VMEM((n, 1, BLK), i32),
            pltpu.SMEM((n, 1, BLK), i32),
            pltpu.VMEM((2, HD), f32),
            pltpu.VMEM((2, HD), f32),
            pltpu.VMEM((n, 2, HD), f32),
            pltpu.VMEM((ndp, 2, HD), f32),
            dma((4, n)), dma((4, n)), dma((n,)), dma((n,)), dma((3, n)), dma((3, n)),
            dma((n,)), dma((n,)), dma((ndp,)), dma((ndp,)), dma((4,)), dma((3,)), dma,
        ],
        compiler_params=pltpu.CompilerParams(
            collective_id=0, has_side_effects=True, vmem_limit_bytes=62 * 2**20),
        cost_estimate=pl.CostEstimate(
            flops=10 * HD * length * length // 2, bytes_accessed=14 * length * HD, transcendentals=length * length // 2),
        name="attention_backward",
    )(q_raw, k_raw, grad_out, values, segment_ids, row_plan, q_gain.reshape(1, HD), k_gain.reshape(1, HD))
    oq, ok, ov, gq, gk = pl.pallas_call(
        hand_over,
        out_shape=(big, big, big, small, small),
        in_specs=[hbm] * 3 + [vmem] * 2,
        out_specs=(hbm, hbm, hbm, vmem, vmem),
        scratch_shapes=[pltpu.VMEM((3,) + q_raw.shape[1:], bf), dma((2, 3, 2))],
        name="hand_over",
    )(oq, ok, ov, gq, gk)
    return oq, ok, ov, gq.reshape(HD), gk.reshape(HD)


def solution(mesh):
    rows = P("dp", "seq", None)
    n = mesh.shape["seq"]
    ny = 4
    return jax.shard_map(
        functools.partial(on_device, n // ny, ny, mesh.shape["dp"]),
        mesh=mesh,
        in_specs=(rows, rows, rows, rows, P("dp", "seq"), P("dp", "seq"), P(), P()),
        out_specs=(rows, rows, rows, P(), P()),
        check_vma=False,
    )
```

```python
import functools
import jax
import jax.numpy as jnp
from jax import lax
from jax.experimental import pallas as pl
from jax.experimental.pallas import tpu as pltpu
from jax.sharding import PartitionSpec as P

HD = 128
BLK = 256
BIG = -1e30
LOG2E = 1.4426950408889634
MESH = pl.DeviceIdType.MESH
NT = (((1,), (1,)), ((), ()))


def rows_mean(x):
    return jnp.sum(x, axis=1, keepdims=True) * (1.0 / HD)


def fold(x):
    return x.reshape(x.shape[0] // 8, 8, x.shape[1])


def kernel(
    nx, ny, ndp,
    q_in, k_in, d_in, v_in, seg_in, plan_in, qg_in, kg_in,
    oq, ok, ov, gq_out, gk_out,
    rq, rk, rd, rv, meta_src, meta, fq, fk, fn,
    qaug, kaug, k_t, dor, vr,
    wbuf, inv_ref, dp_a, dp_b, dvf, dkf, stage,
    idx_v, idx_s, gpart, gsum, gbuf1, gbuf2,
    in_send, in_recv, meta_send, meta_recv, out_send, out_recv,
    g1_send, g1_recv, g2_send, g2_recv, loc_sem, oloc_sem, idx_sem,
):
    n = nx * ny
    length = n * BLK
    half = n // 2
    dp = lax.axis_index("dp")
    me = lax.axis_index("seq")
    mx, my = me // ny, me % ny
    factor = HD ** (-0.5)

    def peer_of(o):
        return ((mx + nx - o // ny) % nx) * ny + (my + ny - o % ny) % ny

    def source_of(o):
        return ((mx + o // ny) % nx) * ny + (my + o % ny) % ny

    def stride(o):
        return (o * (7 + 2 * (dp % 2))) % n

    def mixed(o):
        return peer_of(stride(o))

    barrier = pltpu.get_barrier_semaphore()

    def greet(o, c):
        pl.semaphore_signal(barrier, inc=1, device_id=(dp, peer_of(o)), device_id_type=MESH)
        return c

    def greet_dp(o, c):
        pl.semaphore_signal(barrier, inc=1, device_id=((dp + o) % ndp, me), device_id_type=MESH)
        return c

    lax.fori_loop(1, n, greet, 0)
    lax.fori_loop(1, ndp, greet_dp, 0)

    own_rows = pl.ds(pl.multiple_of(me * BLK, BLK), BLK)
    own_cols = pl.ds(pl.multiple_of(me * HD, HD), HD)
    ins = ((k_in, rk), (q_in, rq), (d_in, rd), (v_in, rv))

    def chunk(p):
        return pl.ds(pl.multiple_of(p * BLK, BLK), BLK)

    def local_in(a):
        src, dst = ins[a]
        return pltpu.make_async_copy(src.at[0, :, own_cols], dst.at[own_rows, :], loc_sem.at[a])

    for a in range(4):
        local_in(a).start()
    meta_src[0:1, :] = seg_in[...]
    meta_src[1:2, :] = plan_in[...]
    meta[me] = meta_src[...]
    pl.semaphore_wait(barrier, n - 1 + ndp - 1)

    def send_meta(o):
        return pltpu.make_async_remote_copy(
            src_ref=meta_src, dst_ref=meta.at[me], send_sem=meta_send.at[o], recv_sem=meta_recv.at[o],
            device_id=(dp, peer_of(o)), device_id_type=MESH)

    def send_in(a, o):
        src, dst = ins[a]
        p = peer_of(o)
        return pltpu.make_async_remote_copy(
            src_ref=src.at[0, :, pl.ds(pl.multiple_of(p * HD, HD), HD)], dst_ref=dst.at[own_rows, :],
            send_sem=in_send.at[a, o], recv_sem=in_recv.at[a, o],
            device_id=(dp, p), device_id_type=MESH)

    def loop(lo, hi, body):
        def step(i, c):
            body(i)
            return c
        lax.fori_loop(lo, hi, step, 0)

    loop(1, n, lambda o: send_meta(o).start())
    for a in range(4):
        loop(1, n, lambda o, a=a: send_in(a, stride(o)).start())

    loop(1, n, lambda o: send_meta(o).wait())
    ids = meta[:, 0, :]
    starts = [jnp.int32(0)] + [jnp.sum((ids < c).astype(jnp.int32)) for c in (1, 2, 3)]
    ends = starts[1:] + [jnp.int32(length)]
    shift = jnp.int32(0)
    for lo, hi in zip(starts, ends):
        shift = shift + jnp.where(hi - lo == length // 2, lo, 0)

    slip = lax.rem(shift, BLK)
    lead = lax.div(shift, BLK)

    def kin(tile, c):
        outside = jnp.where(lax.rem(tile + n - lead, n) >= half, half, 0)
        return lax.rem(lead + outside + c, n)

    lane = lax.broadcasted_iota(jnp.int32, (64, BLK), 1)
    sub = lax.broadcasted_iota(jnp.int32, (64, BLK), 0)

    def invert(d):
        row = jnp.zeros((1, BLK), jnp.int32)
        for g in range(BLK // 64):
            want = sub + (d * BLK + g * 64)
            acc = jnp.zeros((64, BLK), jnp.int32)
            for src in range(n):
                acc = jnp.maximum(acc, jnp.where(meta[src, 1:2, :] == want, lane + src * BLK, 0))
            col = jnp.max(acc, axis=1, keepdims=True)
            row = jnp.maximum(row, jnp.max(jnp.where(lane == sub + g * 64, col, 0), axis=0, keepdims=True))
        row = row - slip
        idx_v[d] = jnp.where(row < 0, row + length, row)

    loop(0, n, invert)
    to_smem = pltpu.make_async_copy(idx_v, idx_s, idx_sem)
    to_smem.start()

    def on_arrival(a, take, tile):
        def get(o):
            send_in(a, o).wait_recv()
            p = source_of(o)
            take(p, p)

            @pl.when(p == 0)
            def _():
                take(0, n)

        local_in(a).wait()
        take(me, me)

        @pl.when(me == 0)
        def _():
            take(0, n)

        loop(1, ny, get)

        def one(k):
            @pl.when((k % ny == ny - 1) & (k < n - ny))
            def _():
                loop(k + 1, k + 1 + ny, get)
            tile(((mx + k // ny) % nx) * ny + k % ny, k)

        loop(0, n, one)

    def rows_of(u):
        return pl.ds(u * BLK + slip, BLK)

    wide_lane = lax.broadcasted_iota(jnp.int32, (BLK, HD), 1)
    wide_sub = lax.broadcasted_iota(jnp.int32, (BLK, HD), 0)

    def clip_of(u):
        pos = wide_sub + (slip + u * BLK)
        pos = jnp.where(pos >= length, pos - length, pos)
        one = lambda b: jnp.where(pos >= b, 1, 0)
        return one(starts[1]) + one(starts[2]) + one(starts[3])

    def hat_of(x):
        rms = lax.rsqrt(rows_mean(x * x) + 1e-06)
        return x * rms, rms

    def norm_chunk(src, full, gain, o, to):
        x = src[chunk(o), :].astype(jnp.float32)
        full[chunk(to), :] = x
        hat, _ = hat_of(x)
        fn[chunk(to), :] = (hat * gain[...]).astype(jnp.bfloat16).astype(jnp.float32)

    def prep_k(b):
        x = fn[rows_of(b), :]
        kaug[b, :, 0:HD] = x.astype(jnp.bfloat16)
        other = jnp.where(wide_lane == clip_of(b), 0.0, jnp.where(wide_lane < 4, BIG, 0.0))
        kaug[b, :, HD:2 * HD] = other.astype(jnp.bfloat16)
        k_t[b] = x.T.astype(jnp.bfloat16)

    on_arrival(0, lambda o, to: norm_chunk(rk, fk, kg_in, o, to), lambda b, k: prep_k(b))

    def prep_q(b):
        qaug[b, :, 0:HD] = fn[rows_of(b), :].astype(jnp.bfloat16)
        qaug[b, :, HD:2 * HD] = jnp.where(wide_lane == clip_of(b), 1.0, 0.0).astype(jnp.bfloat16)

    scale = factor * LOG2E

    def weigh(t):
        queries = qaug[t]
        top = None
        for c in range(half):
            s = lax.dot_general(kaug[kin(t, c)], queries, NT, preferred_element_type=jnp.float32)
            wbuf[t, c] = s
            m = jnp.max(fold(s), axis=0)
            top = m if top is None else jnp.maximum(top, m)
        top = jnp.max(top, axis=0, keepdims=True) * scale
        total = jnp.zeros((8, BLK), jnp.float32)
        for c in range(half):
            w = jnp.exp2(wbuf[t, c] * scale - top)
            wbuf[t, c] = w
            total = total + jnp.sum(fold(w), axis=0)
        inv_ref[t] = 1.0 / jnp.sum(total, axis=0, keepdims=True)

    def take_q(b, k):
        prep_q(b)
        weigh(b)

    on_arrival(1, lambda o, to: norm_chunk(rq, fq, qg_in, o, to), take_q)

    def widen(src, o, to):
        fn[chunk(to), :] = src[chunk(o), :].astype(jnp.float32)

    def prep_d(b):
        dor[b] = fn[rows_of(b), :].astype(jnp.bfloat16)

    on_arrival(2, lambda o, to: widen(rd, o, to), lambda b, k: prep_d(b))

    def place(b):
        return lax.rem(b + n - lead, half)

    def value_grad(b):
        acc = jnp.zeros((BLK, HD), jnp.float32)
        for j in range(half):
            t = kin(b, j)
            probs = (wbuf[t, place(b)] * inv_ref[t]).astype(jnp.bfloat16)
            acc = acc + jnp.dot(probs, dor[t], preferred_element_type=jnp.float32)
        dvf[chunk(b), :] = acc

    loop(0, n, value_grad)
    to_smem.wait()

    outs = ((rq, ov), (rk, oq), (rd, ok))

    def send_out(a, o):
        src, dst = outs[a]
        p = mixed(o)
        return pltpu.make_async_remote_copy(
            src_ref=src.at[chunk(p), :], dst_ref=dst.at[0, :, own_cols],
            send_sem=out_send.at[a, o], recv_sem=out_recv.at[a, o],
            device_id=(dp, p), device_id_type=MESH)

    def local_out(a):
        src, dst = outs[a]
        return pltpu.make_async_copy(src.at[own_rows, :], dst.at[0, :, own_cols], oloc_sem.at[a])

    def pick(rows, a, p, lo, count):
        for j in range(lo, lo + count):
            stage[j:j + 1, :] = rows[pl.ds(idx_s[p, 0, j], 1), :]
        out = outs[a][0]
        out[pl.ds(pl.multiple_of(p * BLK + lo, 16), count), :] = stage[lo:lo + count, :].astype(jnp.bfloat16)

    def leave(a, o):
        @pl.when(o == 0)
        def _():
            local_out(a).start()

        @pl.when(o != 0)
        def _():
            send_out(a, o).start()

    def take_v(b, k):
        vr[b] = fn[rows_of(b), :].astype(jnp.bfloat16)
        pick(dvf, 0, mixed(k), 0, BLK)
        leave(0, k)

    on_arrival(3, lambda o, to: widen(rv, o, to), take_v)
    gpart[...] = jnp.zeros_like(gpart)

    def denorm(rows, full, b, gain):
        hat, rms = hat_of(full[rows_of(b), :])
        d_norm = rows[chunk(b), :]
        d_hat = d_norm * gain[...]
        rows[chunk(b), :] = rms * (d_hat - hat * rows_mean(d_hat * hat))
        return d_norm, hat

    def denorm_q(b, valid=True):
        d_norm, hat = denorm(fn, fq, b, qg_in)
        normed = qaug[b, :, 0:HD].astype(jnp.float32)
        gpart[0:1, :] += jnp.where(valid, jnp.sum(d_norm * hat, axis=0, keepdims=True), 0.0)
        gpart[1:2, :] += jnp.where(valid, jnp.sum(d_norm * normed, axis=0, keepdims=True), 0.0)

    part = BLK // half

    def value_dot(t, c):
        return lax.dot_general(vr[kin(t, c)], dor[t], NT, preferred_element_type=jnp.float32)

    def weighted(d, t, c):
        return jnp.sum(fold(d * wbuf[t, c]), axis=0)

    def score_grad(t, acc, now, t_next, later):
        denorm_q((t + n - 1) % n, t > 0)
        delta = jnp.sum(acc, axis=0, keepdims=True) * inv_ref[t]
        scaled = inv_ref[t] * factor
        dq_t = jnp.zeros((HD, BLK), jnp.float32)
        acc = jnp.zeros((8, BLK), jnp.float32)
        for c in range(half):
            d = value_dot(t_next, c)
            ds = (wbuf[t, c] * scaled) * (now[c] - delta)
            wbuf[t, c] = ds
            dq_t = dq_t + jnp.dot(k_t[kin(t, c)], ds.astype(jnp.bfloat16), preferred_element_type=jnp.float32)
            later[c] = d
            acc = acc + weighted(d, t_next, c)
        fn[chunk(t), :] = dq_t.T
        return acc

    acc = jnp.zeros((8, BLK), jnp.float32)
    for c in range(half):
        d = value_dot(0, c)
        dp_a[c] = d
        acc = acc + weighted(d, 0, c)

    def two(i, acc):
        t = 2 * i
        acc = score_grad(t, acc, dp_a, t + 1, dp_b)
        return score_grad(t + 1, acc, dp_b, (t + 2) % n, dp_a)

    lax.fori_loop(0, n // 2, two, acc)
    denorm_q(n - 1)
    gpart[1:2, :] = gpart[1:2, :] / kg_in[...]
    dkf[chunk(n - 1), :] = jnp.zeros((BLK, HD), jnp.float32)

    gbuf1[me] = gpart[...]

    def send_g1(o):
        return pltpu.make_async_remote_copy(
            src_ref=gpart, dst_ref=gbuf1.at[me], send_sem=g1_send.at[o], recv_sem=g1_recv.at[o],
            device_id=(dp, peer_of(o)), device_id_type=MESH)

    def send_g2(o):
        return pltpu.make_async_remote_copy(
            src_ref=gsum, dst_ref=gbuf2.at[dp], send_sem=g2_send.at[o], recv_sem=g2_recv.at[o],
            device_id=((dp + o) % ndp, me), device_id_type=MESH)

    loop(1, n, lambda o: send_g1(o).start())

    def key_grad(b):
        dest = mixed(b)
        denorm(dkf, fk, (b + n - 1) % n, kg_in)
        acc = jnp.zeros((BLK, HD), jnp.float32)
        for j in range(half):
            t = kin(b, j)
            ds = wbuf[t, place(b)].astype(jnp.bfloat16)
            acc = acc + jnp.dot(ds, qaug[t, :, 0:HD], preferred_element_type=jnp.float32)
            pick(fn, 1, dest, j * part, part)
        dkf[chunk(b), :] = acc
        leave(1, b)

    loop(0, n, key_grad)
    denorm(dkf, fk, n - 1, kg_in)

    def key_rows(o):
        pick(dkf, 2, mixed(o), 0, BLK)
        leave(2, o)

    loop(1, n, lambda o: send_g1(o).wait())
    gsum[...] = jnp.sum(gbuf1[...], axis=0)
    gbuf2[dp] = gsum[...]
    loop(1, ndp, lambda o: send_g2(o).start())
    loop(0, n, key_rows)

    loop(1, ndp, lambda o: send_g2(o).wait())
    grads = jnp.sum(gbuf2[...], axis=0)
    gq_out[...] = grads[0:1, :]
    gk_out[...] = grads[1:2, :]

    for a in range(4):
        loop(1, n, lambda o, a=a: send_in(a, o).wait_send())
    for a in range(3):
        loop(1, n, lambda o, a=a: send_out(a, o).wait())
    for a in range(3):
        local_out(a).wait()


def hand_over(q, k, v, gq, gk, oq, ok, ov, gq_out, gk_out, held, sem):
    pairs = ((q, oq), (k, ok), (v, ov))
    parts = 4
    size = q.shape[1] // parts

    def move(a, part):
        rows = pl.ds(part * size, size)
        src, dst = pairs[a]
        return (pltpu.make_async_copy(src.at[0, rows, :], held.at[a, rows, :], sem.at[0, a, part]),
                pltpu.make_async_copy(held.at[a, rows, :], dst.at[0, rows, :], sem.at[1, a, part]))

    moves = [move(a, part) for a in range(3) for part in range(parts)]
    for get, _ in moves:
        get.start()
    gq_out[...] = gq[...]
    gk_out[...] = gk[...]
    for get, put in moves:
        get.wait()
        put.start()
    for _, put in moves:
        put.wait()


def on_device(nx, ny, ndp, q_raw, k_raw, values, grad_out, segment_ids, row_plan, q_gain, k_gain):
    n = nx * ny
    length = n * BLK
    bf, f32, i32 = jnp.bfloat16, jnp.float32, jnp.int32
    dma = pltpu.SemaphoreType.DMA
    hbm = pl.BlockSpec(memory_space=pl.ANY)
    vmem = pl.BlockSpec(memory_space=pltpu.VMEM)
    big = jax.ShapeDtypeStruct(q_raw.shape, bf)
    small = jax.ShapeDtypeStruct((1, HD), f32)
    half = n // 2
    oq, ok, ov, gq, gk = pl.pallas_call(
        functools.partial(kernel, nx, ny, ndp),
        out_shape=(big, big, big, small, small),
        in_specs=[hbm] * 4 + [vmem] * 4,
        out_specs=(hbm, hbm, hbm, vmem, vmem),
        scratch_shapes=[
            pltpu.VMEM((length, HD), bf),
            pltpu.VMEM((length, HD), bf),
            pltpu.VMEM((length, HD), bf),
            pltpu.VMEM((length, HD), bf),
            pltpu.VMEM((2, BLK), i32),
            pltpu.VMEM((n, 2, BLK), i32),
            pltpu.VMEM((length + BLK, HD), f32),
            pltpu.VMEM((length + BLK, HD), f32),
            pltpu.VMEM((length + BLK, HD), f32),
            pltpu.VMEM((n, BLK, 2 * HD), bf),
            pltpu.VMEM((n, BLK, 2 * HD), bf),
            pltpu.VMEM((n, HD, BLK), bf),
            pltpu.VMEM((n, BLK, HD), bf),
            pltpu.VMEM((n, BLK, HD), bf),
            pltpu.VMEM((n, half, BLK, BLK), f32),
            pltpu.VMEM((n, 1, BLK), f32),
            pltpu.VMEM((half, BLK, BLK), f32),
            pltpu.VMEM((half, BLK, BLK), f32),
            pltpu.VMEM((length, HD), f32),
            pltpu.VMEM((length, HD), f32),
            pltpu.VMEM((BLK, HD), f32),
            pltpu.VMEM((n, 1, BLK), i32),
            pltpu.SMEM((n, 1, BLK), i32),
            pltpu.VMEM((2, HD), f32),
            pltpu.VMEM((2, HD), f32),
            pltpu.VMEM((n, 2, HD), f32),
            pltpu.VMEM((ndp, 2, HD), f32),
            dma((4, n)), dma((4, n)), dma((n,)), dma((n,)), dma((3, n)), dma((3, n)),
            dma((n,)), dma((n,)), dma((ndp,)), dma((ndp,)), dma((4,)), dma((3,)), dma,
        ],
        compiler_params=pltpu.CompilerParams(
            collective_id=0, has_side_effects=True, vmem_limit_bytes=62 * 2**20),
        cost_estimate=pl.CostEstimate(
            flops=10 * HD * length * length // 2, bytes_accessed=14 * length * HD, transcendentals=length * length // 2),
        name="attention_backward",
    )(q_raw, k_raw, grad_out, values, segment_ids, row_plan, q_gain.reshape(1, HD), k_gain.reshape(1, HD))
    oq, ok, ov, gq, gk = pl.pallas_call(
        hand_over,
        out_shape=(big, big, big, small, small),
        in_specs=[hbm] * 3 + [vmem] * 2,
        out_specs=(hbm, hbm, hbm, vmem, vmem),
        scratch_shapes=[pltpu.VMEM((3,) + q_raw.shape[1:], bf), dma((2, 3, 4))],
        name="hand_over",
    )(oq, ok, ov, gq, gk)
    return oq, ok, ov, gq.reshape(HD), gk.reshape(HD)


def solution(mesh):
    rows = P("dp", "seq", None)
    n = mesh.shape["seq"]
    ny = 4
    return jax.shard_map(
        functools.partial(on_device, n // ny, ny, mesh.shape["dp"]),
        mesh=mesh,
        in_specs=(rows, rows, rows, rows, P("dp", "seq"), P("dp", "seq"), P(), P()),
        out_specs=(rows, rows, rows, P(), P()),
        check_vma=False,
    )
```
